32 devices in a mesh: groups: 2 (over y), adapter: 4 (over z), tensor: 4 (over x, core).
Axes of the slice: x: 2, y: 2, z: 4, core: 2. Of those that a mesh axis runs over, the one named last changes fastest.
Arguments:
- tokens: bfloat16 [768, 8192], P(('groups', 'adapter'), 'tensor'), parts along dimension 0, may hold values from -6 to 6
- query_value_weight: bfloat16 [8192, 9216], P('tensor', 'adapter'), may hold values from -0.0625 to 0.0625
- adapter_down_factors: bfloat16 [8, 8192, 128], P('adapter', 'tensor'), may hold values from -0.0625 to 0.0625
- adapter_query_factors: bfloat16 [8, 64, 8192], P('adapter'), may hold values from -0.75 to 0.75
- adapter_value_factors: bfloat16 [8, 64, 1024], P('adapter'), may hold values from -0.75 to 0.75
- adapter_index_rows: int32 [768], P(('groups', 'adapter')), parts along dimension 0, may hold values from 0 to 7, as said below
Outputs:
- qv_out: bfloat16 [768, 9216], P(('groups', 'tensor'), 'adapter'), parts along dimension 0
The draws below stay inside these ranges and needn't reach their ends.
There are 2 independent parts, one for each index of `groups`. The reference program is written for one: setup_inputs(seed, part) draws one part's arguments, and reference() takes and returns one part's arrays. A program takes and returns all parts, laid end to end along the dimension named above; an argument that names none is the same for every part. Nothing has to cross between parts.
Inputs may be any that keep to these rules, and one draw needn't show every extreme that they name: `adapter_index_rows`: the owner of adapter k is k // 2. In every aligned block of 96 rows, at most 48 rows name adapters of one owner, and one owner, the same in every block,, the same in every block, is named by exactly 48 rows in every block.
All inputs are finite; a program needn't handle non-finite values.
Results may differ from the reference program's by a relative error of at most 0.0037.
Values may be sent and summed in bfloat16 or wider, within the bound.
A program may use at most 64 MiB of HBM per device.

```python
import jax
import jax.numpy as jnp
from jax import lax

MODEL_WIDTH = 8192
KVHEADS = 8
HEAD = 128
ADAPTER_RANK = 64
ADP_DEV = 2
ROW_DEV = 96
ROWS = 384
ADAPTER_TOTAL = 8
QUERY_WIDTH = 8192
VALUE_WIDTH = 1024
DQV = 9216
CAP = 48


def draw_adapter_index_rows(key, part):
    key = jax.random.fold_in(key, 11)
    blocks = ROWS // ROW_DEV
    key_hot, key_blocks = jax.random.split(key)
    hottest = jax.random.randint(key_hot, (), 0, blocks).astype(jnp.int32)
    others = jnp.arange(blocks - 1, dtype=jnp.int32)
    others = others + (others >= hottest).astype(jnp.int32)
    pool = jnp.repeat(others, CAP - 1)

    def one_block(block_key):
        key_rest, key_order, key_inner = jax.random.split(block_key, 3)
        rest = jax.random.permutation(key_rest, pool)[:ROW_DEV - CAP]
        owners = jnp.concatenate([jnp.zeros((CAP,), jnp.int32) + hottest, rest])
        owners = jax.random.permutation(key_order, owners)
        inner = jax.random.randint(key_inner, (ROW_DEV,), 0, ADP_DEV).astype(jnp.int32)
        return owners * ADP_DEV + inner
    block_keys = jax.random.split(key_blocks, blocks)
    return jax.vmap(one_block)(block_keys).reshape(ROWS).astype(jnp.int32)


def steps_of(own_key, shape, cuts, low, largest):
    loudness, own = 1.0, jax.random.fold_in(own_key, 6)
    for axis_at, parts in cuts:
        steps = jnp.exp(jax.random.uniform(jax.random.fold_in(own, axis_at), (parts,), jnp.float32, low / len(cuts), largest / len(cuts)))
        loudness = loudness * jnp.repeat(steps, shape[axis_at] // parts).reshape([-1 if axis == axis_at else 1 for axis in range(len(shape))])
    return loudness


def bell_draw(key, dims, scale, bound, cuts=(), held_as=jnp.bfloat16):
    result = jax.random.normal(key, dims, jnp.float32) * scale
    if len(cuts) > 0:
        result = steps_of(key, dims, cuts, -0.22, 0.18) * result
    return jnp.clip(result, min=-bound, max=bound).astype(held_as)


def setup_inputs(seed: int = 0, part: int = 0) -> dict:
    splits = jax.random.split(jax.random.key(seed), 7)
    part_keys = jax.random.split(jax.random.fold_in(splits[6], part), 7)
    tokens = bell_draw(part_keys[0], (ROWS, MODEL_WIDTH), 1.0, 6.0, ((0, 4), (1, 4)))
    query_value_weight = bell_draw(splits[1], (MODEL_WIDTH, DQV), MODEL_WIDTH ** -0.5, 0.0625, ((0, 4), (1, 4)))
    adapter_down_factors = bell_draw(splits[2], (ADAPTER_TOTAL, MODEL_WIDTH, 2 * ADAPTER_RANK), MODEL_WIDTH ** -0.5, 0.0625, ((0, 4), (1, 4)))
    adapter_query_factors = bell_draw(splits[3], (ADAPTER_TOTAL, ADAPTER_RANK, QUERY_WIDTH), ADAPTER_RANK ** -0.5, 0.75, ((0, 4),))
    adapter_value_factors = bell_draw(splits[4], (ADAPTER_TOTAL, ADAPTER_RANK, VALUE_WIDTH), ADAPTER_RANK ** -0.5, 0.75, ((0, 4),))
    adapter_index_rows = draw_adapter_index_rows(jax.random.fold_in(jax.random.fold_in(splits[6], part), 71), part)
    return {"tokens": tokens, "query_value_weight": query_value_weight, "adapter_down_factors": adapter_down_factors, "adapter_query_factors": adapter_query_factors, "adapter_value_factors": adapter_value_factors, "adapter_index_rows": adapter_index_rows}


def reference(tokens, query_value_weight, adapter_down_factors, adapter_query_factors, adapter_value_factors, adapter_index_rows):
    base = jnp.dot(tokens, query_value_weight, preferred_element_type=jnp.float32)

    def shrink_step(total, position_index):
        mask = (adapter_index_rows == position_index)[:, None]
        adapter_term = jnp.dot(tokens, adapter_down_factors[position_index], preferred_element_type=jnp.float32)
        return total + jnp.where(mask, adapter_term, jnp.zeros_like(adapter_term)), None

    start_low = jnp.zeros((ROWS, 2 * ADAPTER_RANK), jnp.float32)
    reduced_rows, _ = lax.scan(shrink_step, start_low, jnp.arange(ADAPTER_TOTAL, dtype=jnp.int32))
    reduced_rows = (reduced_rows * 0.5).astype(jnp.bfloat16)

    def expand_step(totals, position_index):
        mask = (adapter_index_rows == position_index)[:, None]
        selected_factor = jnp.where(mask, reduced_rows, jnp.zeros_like(reduced_rows))
        query_portion = jnp.dot(selected_factor[:, :ADAPTER_RANK], adapter_query_factors[position_index], preferred_element_type=jnp.float32)
        value_portion = jnp.dot(selected_factor[:, ADAPTER_RANK:], adapter_value_factors[position_index], preferred_element_type=jnp.float32)
        return (totals[0] + query_portion, totals[1] + value_portion), None

    start_up = (jnp.zeros((ROWS, QUERY_WIDTH), jnp.float32), jnp.zeros((ROWS, VALUE_WIDTH), jnp.float32))
    (delta_q, delta_v), _ = lax.scan(expand_step, start_up, jnp.arange(ADAPTER_TOTAL, dtype=jnp.int32))
    delta_q = delta_q.astype(jnp.bfloat16).reshape(ROWS, KVHEADS, QUERY_WIDTH // KVHEADS)
    delta_v = delta_v.astype(jnp.bfloat16).reshape(ROWS, KVHEADS, HEAD)
    delta = jnp.concatenate([delta_q, delta_v], axis=2).reshape(ROWS, DQV)
    return (base + delta.astype(jnp.float32)).astype(jnp.bfloat16)
```

```python
import jax
import jax.numpy as jnp
from jax import lax
from jax.experimental import pallas as pl
from jax.experimental.pallas import tpu as pltpu
from jax.sharding import PartitionSpec as P

KVHEADS = 8


adapter_scale = 0.5


def slot_table(hit, capacity):
    counts = jnp.cumsum(hit.astype(jnp.int32), axis=-1) - 1
    places = jnp.arange(capacity, dtype=jnp.int32)
    match = hit[..., None, :] & (counts[..., None, :] == places[:, None])
    column = jnp.arange(hit.shape[-1], dtype=jnp.int32)
    row_of = jnp.sum(jnp.where(match, column, 0), axis=-1)
    filled = jnp.any(match, axis=-1)
    return (row_of, filled)


def on_device(
    tokens,
    query_value_weight,
    adapter_down_factors,
    adapter_query_factors,
    adapter_value_factors,
    adapter_index_rows,
):
    owners_n = lax.axis_size("adapter")
    tensor_n = lax.axis_size("tensor")
    owner_self = lax.axis_index("adapter")
    tensor_self = lax.axis_index("tensor")
    row_dev = tokens.shape[0]
    local_row_count = adapter_down_factors.shape[0]
    value_rank_slice = adapter_down_factors.shape[2]
    query_rank_slice = value_rank_slice // 2
    capacity = max(2, min(4 * row_dev // owners_n, row_dev // 2))
    group_src = owners_n // tensor_n
    block_cols = query_value_weight.shape[1]
    all_ids = lax.all_gather(adapter_index_rows, "adapter", axis=0, tiled=True).reshape(
        owners_n, row_dev
    )
    owners_all = all_ids // local_row_count
    gathered = lax.all_gather(tokens, "adapter", axis=0, tiled=True)
    base = lax.psum_scatter(
        jnp.dot(gathered, query_value_weight, preferred_element_type=jnp.float32),
        "tensor",
        scatter_dimension=0,
        tiled=True,
    )
    slot_row, slot_ok = slot_table(owners_all == owner_self, capacity)
    slot_ids = jnp.take_along_axis(all_ids, slot_row, axis=1)
    local_pick = (slot_ids - owner_self * local_row_count)[..., None] == jnp.arange(
        local_row_count, dtype=jnp.int32
    )
    select = (local_pick & slot_ok[..., None]).astype(jnp.float32)
    targets = jnp.arange(owners_n, dtype=jnp.int32)[:, None]
    send_row, send_ok = slot_table(
        (adapter_index_rows // local_row_count)[None, :] == targets, capacity
    )
    outgoing = jnp.where(send_ok[..., None], tokens[send_row], jnp.zeros((), tokens.dtype))
    dense = jnp.einsum(
        "scd,kdq->sckq",
        lax.all_to_all(outgoing, "adapter", split_axis=0, concat_axis=0, tiled=True),
        adapter_down_factors,
        preferred_element_type=jnp.float32,
    )
    partial_low = jnp.sum(dense * select[..., None], axis=2)
    accumulated_sum = lax.psum(partial_low, "tensor")
    accumulated_sum = lax.dynamic_slice_in_dim(
        accumulated_sum, tensor_self * group_src, group_src, 0
    )
    reduced_rows = (accumulated_sum * adapter_scale).astype(jnp.bfloat16)
    mine = lax.dynamic_slice_in_dim(select, tensor_self * group_src, group_src, 0).astype(
        jnp.bfloat16
    )
    slots_n = group_src * capacity
    broadcast_rows = (mine[..., None] * reduced_rows[..., None, :]).reshape(
        slots_n, local_row_count, value_rank_slice
    )
    up_query = jnp.einsum(
        "mwn,wnq->mq",
        broadcast_rows[..., :query_rank_slice],
        adapter_query_factors,
        preferred_element_type=jnp.float32,
    )
    up_value = jnp.einsum(
        "mwn,wnq->mq",
        broadcast_rows[..., query_rank_slice:],
        adapter_value_factors,
        preferred_element_type=jnp.float32,
    )
    delta = jnp.concatenate(
        [
            up_query.astype(jnp.bfloat16).reshape(slots_n, KVHEADS, -1),
            up_value.astype(jnp.bfloat16).reshape(slots_n, KVHEADS, -1),
        ],
        axis=2,
    )
    delta = delta.reshape(slots_n, owners_n, block_cols).transpose(1, 0, 2)
    returned = lax.all_to_all(delta, "adapter", split_axis=0, concat_axis=0, tiled=True).reshape(
        owners_n * slots_n, block_cols
    )
    mine_owner = lax.dynamic_slice_in_dim(owners_all, tensor_self * group_src, group_src, 0)
    owner_hit = mine_owner[:, None, :] == jnp.arange(owners_n, dtype=jnp.int32)[None, :, None]
    running = jnp.cumsum(owner_hit.astype(jnp.int32), axis=-1) - 1
    place = jnp.sum(jnp.where(owner_hit, running, 0), axis=1)
    source_off = jnp.arange(group_src, dtype=jnp.int32)[:, None] * capacity
    lookup = (mine_owner * slots_n + source_off + place).reshape(-1)
    delta_rows = jnp.take(returned, lookup, axis=0)
    return (base + delta_rows.astype(jnp.float32)).astype(jnp.bfloat16)


MESH = pl.DeviceIdType.MESH
ZN = 4


def remote(src, dst, send_sem, recv_sem, device):
    return pltpu.make_async_remote_copy(
        src_ref=src,
        dst_ref=dst,
        send_sem=send_sem,
        recv_sem=recv_sem,
        device_id=device,
        device_id_type=MESH,
    )


def fused_kernel(
    tok_ref, w_ref, down_ref, bq_ref, bv_ref, ids_ref, out_ref,
    x, wd, send, recv, base, low_send, low_recv, low_z, ball, ids,
    load_sem, own_sem, right_s, left_s, x_r, ids_s, ids_r, part_s, part_r,
    low_s, low_r, lz_s, lz_r, bqz_s, bqz_r, bvz_s, bvz_r, plane_s, plane_r,
):
    g = lax.axis_index("groups")
    a = lax.axis_index("adapter")
    t = lax.axis_index("tensor")
    cols = w_ref.shape[1]
    qcols = bq_ref.shape[2] // ZN
    vcols = bv_ref.shape[2] // ZN
    rank = bq_ref.shape[1]
    rows = tok_ref.shape[0]
    groups_here = KVHEADS // ZN
    qg, vg = qcols // groups_here, vcols // groups_here
    zdev = [lax.rem(a + d, ZN) for d in range(ZN)]
    tdev = [lax.rem(t + d, ZN) for d in range(ZN)]
    xpeer = lax.rem(t + 2, ZN)
    core = lax.rem(t, 2)
    sibling = t + 1 - 2 * core

    loads = [
        pltpu.make_async_copy(w_ref, wd.at[:, pl.ds(0, cols)], load_sem.at[0]),
        pltpu.make_async_copy(down_ref.at[0], wd.at[:, pl.ds(cols, 2 * rank)], load_sem.at[1]),
        pltpu.make_async_copy(
            down_ref.at[1], wd.at[:, pl.ds(cols + 2 * rank, 2 * rank)], load_sem.at[2]
        ),
        pltpu.make_async_copy(tok_ref, x.at[a], load_sem.at[3]),
    ]
    for copy in loads:
        copy.start()
    own_q = pl.ds(pl.multiple_of(a * qcols, 128), qcols)
    own_v = pl.ds(pl.multiple_of(a * vcols, 128), vcols)
    owns = []
    for k in range(2):
        at = pl.ds(k * rank, rank)
        owns.append(pltpu.make_async_copy(
            bq_ref.at[k, :, own_q], ball.at[ZN - 1, at, pl.ds(0, qcols)], own_sem.at[2 * k]))
        owns.append(pltpu.make_async_copy(
            bv_ref.at[k, :, own_v], ball.at[ZN - 1, at, pl.ds(qcols, vcols)], own_sem.at[2 * k + 1]))
    for copy in owns:
        copy.start()
    ids[pl.ds(a, 1)] = ids_ref[...][None]

    barrier = pltpu.get_barrier_semaphore()
    for d in range(1, ZN):
        pl.semaphore_signal(barrier, inc=1, device_id={"adapter": zdev[d]}, device_id_type=MESH)
        pl.semaphore_signal(barrier, inc=1, device_id={"tensor": tdev[d]}, device_id_type=MESH)
    pl.semaphore_signal(barrier, inc=1, device_id={"groups": 1 - g}, device_id_type=MESH)
    pl.semaphore_wait(barrier, 2 * ZN - 1)

    def to_right(src, b):
        return remote(src, x.at[b], right_s.at[b], x_r.at[b], {"adapter": lax.rem(a + 1, ZN)})

    def to_left(src, b):
        return remote(src, x.at[b], left_s.at[b], x_r.at[b], {"adapter": lax.rem(a + ZN - 1, ZN)})

    @pl.when(a < ZN - 1)
    def _():
        to_right(tok_ref, a).start()

    @pl.when(a > 0)
    def _():
        to_left(tok_ref, a).start()

    part = ball.shape[1] // (2 * ZN)
    p = 2 * t + g
    p_rows = pl.ds(pl.multiple_of(p * part, part), part)
    k_src = t // 2
    r_src = pl.ds(pl.multiple_of((2 * core + g) * part, part), part)

    def ids_copy(d):
        return remote(ids_ref, ids.at[a], ids_s.at[d], ids_r.at[a], {"adapter": zdev[d]})

    def bq_copy(d):
        at = pl.ds(pl.multiple_of(zdev[d] * qcols, 128), qcols)
        return remote(bq_ref.at[k_src, r_src, at], ball.at[d - 1, p_rows, pl.ds(0, qcols)],
                      bqz_s.at[d], bqz_r.at[d], {"adapter": zdev[d]})

    def bv_copy(d):
        at = pl.ds(pl.multiple_of(zdev[d] * vcols, 128), vcols)
        return remote(bv_ref.at[k_src, r_src, at], ball.at[d - 1, p_rows, pl.ds(qcols, vcols)],
                      bvz_s.at[d], bvz_r.at[d], {"adapter": zdev[d]})

    for d in range(1, ZN):
        ids_copy(d).start()
    for d in range(1, ZN):
        bq_copy(d).start()
        bv_copy(d).start()

    def y_copy():
        ref = ball.at[pl.ds(0, ZN - 1), p_rows, :]
        return remote(ref, ref, plane_s.at[0], plane_r.at[0], {"groups": 1 - g})

    def t_rows(owner_t):
        return ball.at[pl.ds(0, ZN - 1), pl.ds(pl.multiple_of(owner_t * 2 * part, 2 * part), 2 * part), :]

    def x_copy(owner_t):
        ref = t_rows(owner_t)
        return remote(ref, ref, plane_s.at[1], plane_r.at[1], {"tensor": xpeer})

    def core_copy(i, owner_t):
        ref = t_rows(owner_t)
        return remote(ref, ref, plane_s.at[2 + i], plane_r.at[2 + i], {"tensor": sibling})

    def column(b):
        lane = lax.broadcasted_iota(jnp.int32, (rows, 128), 1)
        row = lax.broadcasted_iota(jnp.int32, (rows, 128), 0)
        ids_b = jnp.broadcast_to(ids[b][0:1, :], (rows, 128))
        return jnp.sum(jnp.where(lane == row, ids_b, 0), axis=1, keepdims=True)

    def part_copy(b):
        return remote(send.at[b], recv.at[t], part_s.at[b], part_r.at[t], {"tensor": b})

    def low_copy(b):
        return remote(low_send.at[b], low_recv.at[t], low_s.at[b], low_r.at[t], {"tensor": b})

    tile = 256

    def compute(b):
        both = jnp.dot(x[b], wd[:, cols:], preferred_element_type=jnp.float32)
        id_col = column(b)
        zero = jnp.zeros((rows, 2 * rank), jnp.float32)
        low = jnp.where(id_col == 2 * a, both[:, : 2 * rank], zero)
        low = jnp.where(id_col == 2 * a + 1, both[:, 2 * rank :], low)
        low_send[b] = low

        @pl.when(b != t)
        def _():
            low_copy(b).start()

            @pl.loop(0, cols // tile)
            def _(n):
                at = pl.ds(pl.multiple_of(n * tile, tile), tile)
                send[b, :, at] = jnp.dot(
                    x[b], wd[:, at], preferred_element_type=jnp.float32
                ).astype(jnp.bfloat16)

            part_copy(b).start()

        @pl.when(b == t)
        def _():
            @pl.loop(0, cols // tile)
            def _(n):
                at = pl.ds(pl.multiple_of(n * tile, tile), tile)
                base[:, at] = jnp.dot(x[b], wd[:, at], preferred_element_type=jnp.float32)

    for copy in loads:
        copy.wait()
    compute(a)

    for d in range(1, ZN):
        bq_copy(d).wait_recv()
        bv_copy(d).wait_recv()
    y_copy().start()

    for s in range(1, ZN):
        lo, hi = a - s, a + s

        @pl.when(lo >= 0)
        def _():
            to_right(tok_ref, lo).wait_recv()

            @pl.when(a < ZN - 1)
            def _():
                to_right(x.at[lo], lo).start()

        @pl.when(hi < ZN)
        def _():
            to_left(tok_ref, hi).wait_recv()

            @pl.when(a > 0)
            def _():
                to_left(x.at[hi], hi).start()

        @pl.loop(0, 2)
        def _(way):
            b = a - s + 2 * s * way

            @pl.when((b >= 0) & (b < ZN))
            def _():
                remote(ids_ref, ids.at[b], ids_s.at[1], ids_r.at[b], {"adapter": zdev[1]}).wait_recv()
                compute(b)

        if s == 1:
            y_copy_in = ball.at[pl.ds(0, ZN - 1), pl.ds(pl.multiple_of((2 * t + 1 - g) * part, part), part), :]
            remote(y_copy_in, y_copy_in, plane_s.at[0], plane_r.at[0], {"groups": 1 - g}).wait_recv()
            x_copy(t).start()
        if s == 2:
            x_copy(xpeer).wait_recv()
            core_copy(0, t).start()
            core_copy(1, xpeer).start()

    total = low_send[t]
    for d in range(1, ZN):
        remote(low_send.at[0], low_recv.at[tdev[d]], low_s.at[0], low_r.at[tdev[d]], {"tensor": tdev[d]}).wait_recv()
        total = total + low_recv[tdev[d]]
    low_z[0] = (total * adapter_scale).astype(jnp.bfloat16)

    def lz_copy(d):
        return remote(low_z.at[0], low_z.at[d], lz_s.at[d], lz_r.at[d], {"adapter": zdev[d]})

    for d in range(1, ZN):
        lz_copy(d).start()
    for copy in owns:
        copy.wait()
    core_copy(0, sibling).wait_recv()
    core_copy(1, lax.rem(sibling + 2, ZN)).wait_recv()
    id_col = column(t)
    low = low_z[0].astype(jnp.float32)
    for d in range(1, ZN):
        lz_copy(d).wait_recv()
        low = low + low_z[d].astype(jnp.float32)
    wide = jnp.concatenate([low[:, :rank], low[:, :rank]], axis=1)
    wide_v = jnp.concatenate([low[:, rank:], low[:, rank:]], axis=1)
    second = lax.broadcasted_iota(jnp.int32, (rows, 2 * rank), 1) // rank
    lq, lv = [], []
    for slot in range(ZN):
        owner = zdev[(ZN - 1 - slot) % ZN]
        hit = id_col == 2 * owner + second
        lq.append(jnp.where(hit, wide, 0.0).astype(jnp.bfloat16))
        lv.append(jnp.where(hit, wide_v, 0.0).astype(jnp.bfloat16))
    lq = jnp.concatenate(lq, axis=1)
    lv = jnp.concatenate(lv, axis=1)
    for d in range(1, ZN):
        remote(send.at[0], recv.at[tdev[d]], part_s.at[0], part_r.at[tdev[d]], {"tensor": tdev[d]}).wait_recv()

    def finish(at, low_rows, b_at, width):
        factors = ball[:, :, b_at : b_at + width].reshape(ZN * 2 * rank, width)
        delta = jnp.dot(low_rows, factors, preferred_element_type=jnp.float32)
        val = base[:, at : at + width]
        for d in range(1, ZN):
            val = val + recv[tdev[d], :, at : at + width].astype(jnp.float32)
        delta = delta.astype(jnp.bfloat16).astype(jnp.float32)
        out_ref[:, at : at + width] = (val + delta).astype(jnp.bfloat16)

    for grp in range(groups_here):
        for c in range(qg // 256):
            finish(grp * (qg + vg) + c * 256, lq, grp * qg + c * 256, 256)
        finish(grp * (qg + vg) + qg, lv, qcols + grp * vg, vg)

    @pl.loop(0, ZN)
    def _(b):
        @pl.when((b <= a) & (a < ZN - 1))
        def _():
            to_right(tok_ref, b).wait_send()

        @pl.when((b >= a) & (a > 0))
        def _():
            to_left(tok_ref, b).wait_send()

        @pl.when(b != t)
        def _():
            part_copy(b).wait_send()
            low_copy(b).wait_send()

    for d in range(1, ZN):
        ids_copy(d).wait_send()
        bq_copy(d).wait_send()
        bv_copy(d).wait_send()
        lz_copy(d).wait_send()
    y_copy().wait_send()
    x_copy(t).wait_send()
    core_copy(0, t).wait_send()
    core_copy(1, xpeer).wait_send()


def fused_on_device(tokens, weight, down, bq, bv, index_rows):
    rows, feats = tokens.shape
    cols = weight.shape[1]
    rank2 = down.shape[2]
    ids = jnp.broadcast_to(jnp.pad(index_rows, (0, 128 - rows))[None, :], (8, 128))
    dma = pltpu.SemaphoreType.DMA
    vmem = pltpu.VMEM
    any_spec = pl.BlockSpec(memory_space=pl.ANY)
    return pl.pallas_call(
        fused_kernel,
        out_shape=jax.ShapeDtypeStruct((rows, cols), jnp.bfloat16),
        in_specs=[any_spec] * 5 + [pl.BlockSpec(memory_space=pltpu.VMEM)],
        out_specs=pl.BlockSpec(memory_space=pltpu.VMEM),
        scratch_shapes=[
            vmem((ZN, rows, feats), jnp.bfloat16),
            vmem((feats, cols + 2 * rank2), jnp.bfloat16),
            vmem((ZN, rows, cols), jnp.bfloat16),
            vmem((ZN, rows, cols), jnp.bfloat16),
            vmem((rows, cols), jnp.float32),
            vmem((ZN, rows, rank2), jnp.float32),
            vmem((ZN, rows, rank2), jnp.float32),
            vmem((ZN, rows, rank2), jnp.bfloat16),
            vmem((ZN, rank2, cols), jnp.bfloat16),
            vmem((ZN, 8, 128), jnp.int32),
        ] + [dma((4,))] * 19,
        compiler_params=pltpu.CompilerParams(
            collective_id=0, has_side_effects=True, vmem_limit_bytes=48 * 1024 * 1024
        ),
    )(tokens, weight, down, bq, bv, ids)


def solution(mesh):
    fused = (mesh.shape["groups"], mesh.shape["adapter"], mesh.shape["tensor"]) == (2, ZN, ZN)
    in_specs = (
        P(("groups", "adapter"), "tensor"),
        P("tensor", "adapter"),
        P("adapter", "tensor", None),
        P("adapter", None, None),
        P("adapter", None, None),
        P(("groups", "adapter")),
    )
    out_specs = P(("groups", "tensor"), "adapter")
    return jax.shard_map(
        fused_on_device if fused else on_device,
        mesh=mesh, in_specs=in_specs, out_specs=out_specs, check_vma=False,
    )
```

```python
import jax
import jax.numpy as jnp
from jax import lax
from jax.experimental import pallas as pl
from jax.experimental.pallas import tpu as pltpu
from jax.sharding import PartitionSpec as P

KVHEADS = 8


adapter_scale = 0.5


def slot_table(hit, capacity):
    counts = jnp.cumsum(hit.astype(jnp.int32), axis=-1) - 1
    places = jnp.arange(capacity, dtype=jnp.int32)
    match = hit[..., None, :] & (counts[..., None, :] == places[:, None])
    column = jnp.arange(hit.shape[-1], dtype=jnp.int32)
    row_of = jnp.sum(jnp.where(match, column, 0), axis=-1)
    filled = jnp.any(match, axis=-1)
    return (row_of, filled)


def on_device(
    tokens,
    query_value_weight,
    adapter_down_factors,
    adapter_query_factors,
    adapter_value_factors,
    adapter_index_rows,
):
    owners_n = lax.axis_size("adapter")
    tensor_n = lax.axis_size("tensor")
    owner_self = lax.axis_index("adapter")
    tensor_self = lax.axis_index("tensor")
    row_dev = tokens.shape[0]
    local_row_count = adapter_down_factors.shape[0]
    value_rank_slice = adapter_down_factors.shape[2]
    query_rank_slice = value_rank_slice // 2
    capacity = max(2, min(4 * row_dev // owners_n, row_dev // 2))
    group_src = owners_n // tensor_n
    block_cols = query_value_weight.shape[1]
    all_ids = lax.all_gather(adapter_index_rows, "adapter", axis=0, tiled=True).reshape(
        owners_n, row_dev
    )
    owners_all = all_ids // local_row_count
    gathered = lax.all_gather(tokens, "adapter", axis=0, tiled=True)
    base = lax.psum_scatter(
        jnp.dot(gathered, query_value_weight, preferred_element_type=jnp.float32),
        "tensor",
        scatter_dimension=0,
        tiled=True,
    )
    slot_row, slot_ok = slot_table(owners_all == owner_self, capacity)
    slot_ids = jnp.take_along_axis(all_ids, slot_row, axis=1)
    local_pick = (slot_ids - owner_self * local_row_count)[..., None] == jnp.arange(
        local_row_count, dtype=jnp.int32
    )
    select = (local_pick & slot_ok[..., None]).astype(jnp.float32)
    targets = jnp.arange(owners_n, dtype=jnp.int32)[:, None]
    send_row, send_ok = slot_table(
        (adapter_index_rows // local_row_count)[None, :] == targets, capacity
    )
    outgoing = jnp.where(send_ok[..., None], tokens[send_row], jnp.zeros((), tokens.dtype))
    dense = jnp.einsum(
        "scd,kdq->sckq",
        lax.all_to_all(outgoing, "adapter", split_axis=0, concat_axis=0, tiled=True),
        adapter_down_factors,
        preferred_element_type=jnp.float32,
    )
    partial_low = jnp.sum(dense * select[..., None], axis=2)
    accumulated_sum = lax.psum(partial_low, "tensor")
    accumulated_sum = lax.dynamic_slice_in_dim(
        accumulated_sum, tensor_self * group_src, group_src, 0
    )
    reduced_rows = (accumulated_sum * adapter_scale).astype(jnp.bfloat16)
    mine = lax.dynamic_slice_in_dim(select, tensor_self * group_src, group_src, 0).astype(
        jnp.bfloat16
    )
    slots_n = group_src * capacity
    broadcast_rows = (mine[..., None] * reduced_rows[..., None, :]).reshape(
        slots_n, local_row_count, value_rank_slice
    )
    up_query = jnp.einsum(
        "mwn,wnq->mq",
        broadcast_rows[..., :query_rank_slice],
        adapter_query_factors,
        preferred_element_type=jnp.float32,
    )
    up_value = jnp.einsum(
        "mwn,wnq->mq",
        broadcast_rows[..., query_rank_slice:],
        adapter_value_factors,
        preferred_element_type=jnp.float32,
    )
    delta = jnp.concatenate(
        [
            up_query.astype(jnp.bfloat16).reshape(slots_n, KVHEADS, -1),
            up_value.astype(jnp.bfloat16).reshape(slots_n, KVHEADS, -1),
        ],
        axis=2,
    )
    delta = delta.reshape(slots_n, owners_n, block_cols).transpose(1, 0, 2)
    returned = lax.all_to_all(delta, "adapter", split_axis=0, concat_axis=0, tiled=True).reshape(
        owners_n * slots_n, block_cols
    )
    mine_owner = lax.dynamic_slice_in_dim(owners_all, tensor_self * group_src, group_src, 0)
    owner_hit = mine_owner[:, None, :] == jnp.arange(owners_n, dtype=jnp.int32)[None, :, None]
    running = jnp.cumsum(owner_hit.astype(jnp.int32), axis=-1) - 1
    place = jnp.sum(jnp.where(owner_hit, running, 0), axis=1)
    source_off = jnp.arange(group_src, dtype=jnp.int32)[:, None] * capacity
    lookup = (mine_owner * slots_n + source_off + place).reshape(-1)
    delta_rows = jnp.take(returned, lookup, axis=0)
    return (base + delta_rows.astype(jnp.float32)).astype(jnp.bfloat16)


MESH = pl.DeviceIdType.MESH
CHUNKS = 3
ZN = 4


def remote(src, dst, send_sem, recv_sem, device):
    return pltpu.make_async_remote_copy(
        src_ref=src,
        dst_ref=dst,
        send_sem=send_sem,
        recv_sem=recv_sem,
        device_id=device,
        device_id_type=MESH,
    )


def fused_kernel(
    tok_ref, w_ref, down_ref, bq_ref, bv_ref, ids_ref, out_ref,
    x, wd, pair_send, pair_recv, far_send, far_recv, near_send, near_recv, held, base, low_send, low_recv, low_z, ball, ids,
    load_sem, own_sem, ids_s, ids_r, pair_s, pair_r, far_s, far_r, near_s, near_r,
    low_s, low_r, lz_s, lz_r, bqz_s, bqz_r, bvz_s, bvz_r, plane_s, plane_r, right_s, left_s, x_r,
):
    g = lax.axis_index("groups")
    a = lax.axis_index("adapter")
    t = lax.axis_index("tensor")
    cols = w_ref.shape[1]
    qcols = bq_ref.shape[2] // ZN
    vcols = bv_ref.shape[2] // ZN
    rank = bq_ref.shape[1]
    rows = tok_ref.shape[0]
    groups_here = KVHEADS // ZN
    qg, vg = qcols // groups_here, vcols // groups_here
    zdev = [lax.rem(a + d, ZN) for d in range(ZN)]
    tdev = [lax.rem(t + d, ZN) for d in range(ZN)]
    xpeer = lax.rem(t + 2, ZN)
    core = lax.rem(t, 2)
    sibling = t + 1 - 2 * core

    loads = [
        pltpu.make_async_copy(w_ref, wd.at[:, pl.ds(0, cols)], load_sem.at[0]),
        pltpu.make_async_copy(down_ref.at[0], wd.at[:, pl.ds(cols, 2 * rank)], load_sem.at[1]),
        pltpu.make_async_copy(
            down_ref.at[1], wd.at[:, pl.ds(cols + 2 * rank, 2 * rank)], load_sem.at[2]
        ),
        pltpu.make_async_copy(tok_ref, x.at[a], load_sem.at[3]),
    ]
    for copy in loads:
        copy.start()
    own_q = pl.ds(pl.multiple_of(a * qcols, 128), qcols)
    own_v = pl.ds(pl.multiple_of(a * vcols, 128), vcols)
    owns = []
    for k in range(2):
        at = pl.ds(k * rank, rank)
        owns.append(pltpu.make_async_copy(
            bq_ref.at[k, :, own_q], ball.at[ZN - 1, at, pl.ds(0, qcols)], own_sem.at[2 * k]))
        owns.append(pltpu.make_async_copy(
            bv_ref.at[k, :, own_v], ball.at[ZN - 1, at, pl.ds(qcols, vcols)], own_sem.at[2 * k + 1]))
    for copy in owns:
        copy.start()
    ids[a] = jnp.zeros((8, 128), jnp.int32)
    ids[a, 0:1, 0:rows] = ids_ref[...]

    barrier = pltpu.get_barrier_semaphore()
    for d in range(1, ZN):
        pl.semaphore_signal(barrier, inc=1, device_id={"adapter": zdev[d]}, device_id_type=MESH)
        pl.semaphore_signal(barrier, inc=1, device_id={"tensor": tdev[d]}, device_id_type=MESH)
    pl.semaphore_signal(barrier, inc=1, device_id={"groups": 1 - g}, device_id_type=MESH)
    pl.semaphore_wait(barrier, 2 * ZN - 1)

    step = rows // CHUNKS

    def to_right(src, b, i):
        at = pl.ds(i * step, step)
        return remote(src.at[at], x.at[b, at], right_s.at[b, i], x_r.at[b, i],
                      {"adapter": lax.rem(a + 1, ZN)})

    def to_left(src, b, i):
        at = pl.ds(i * step, step)
        return remote(src.at[at], x.at[b, at], left_s.at[b, i], x_r.at[b, i],
                      {"adapter": lax.rem(a + ZN - 1, ZN)})

    for i in range(CHUNKS):
        @pl.when(a < ZN - 1)
        def _():
            to_right(tok_ref, a, i).start()

        @pl.when(a > 0)
        def _():
            to_left(tok_ref, a, i).start()

    part = ball.shape[1] // (2 * ZN)
    p = 2 * t + g
    p_rows = pl.ds(pl.multiple_of(p * part, part), part)
    k_src = t // 2
    r_src = pl.ds(pl.multiple_of((2 * core + g) * part, part), part)

    def ids_copy(d):
        return remote(ids.at[a], ids.at[a], ids_s.at[d], ids_r.at[a], {"adapter": zdev[d]})

    def bq_copy(d):
        at = pl.ds(pl.multiple_of(zdev[d] * qcols, 128), qcols)
        return remote(bq_ref.at[k_src, r_src, at], ball.at[d - 1, p_rows, pl.ds(0, qcols)],
                      bqz_s.at[d], bqz_r.at[d], {"adapter": zdev[d]})

    def bv_copy(d):
        at = pl.ds(pl.multiple_of(zdev[d] * vcols, 128), vcols)
        return remote(bv_ref.at[k_src, r_src, at], ball.at[d - 1, p_rows, pl.ds(qcols, vcols)],
                      bvz_s.at[d], bvz_r.at[d], {"adapter": zdev[d]})

    for d in range(1, ZN):
        ids_copy(d).start()
    for d in range(1, ZN):
        bq_copy(d).start()
        bv_copy(d).start()

    def y_copy():
        ref = ball.at[pl.ds(0, ZN - 1), p_rows, :]
        return remote(ref, ref, plane_s.at[0], plane_r.at[0], {"groups": 1 - g})

    def t_rows(owner_t):
        return ball.at[pl.ds(0, ZN - 1), pl.ds(pl.multiple_of(owner_t * 2 * part, 2 * part), 2 * part), :]

    def x_copy(owner_t):
        ref = t_rows(owner_t)
        return remote(ref, ref, plane_s.at[1], plane_r.at[1], {"tensor": xpeer})

    def core_copy(i, owner_t):
        ref = t_rows(owner_t)
        return remote(ref, ref, plane_s.at[2 + i], plane_r.at[2 + i], {"tensor": sibling})

    def column(b):
        lane = lax.broadcasted_iota(jnp.int32, (rows, 128), 1)
        row = lax.broadcasted_iota(jnp.int32, (rows, 128), 0)
        ids_b = jnp.broadcast_to(ids[b][0:1, :], (rows, 128))
        return jnp.sum(jnp.where(lane == row, ids_b, 0), axis=1, keepdims=True)

    half = cols // 2
    here = t // 2
    mine_at = pl.ds(pl.multiple_of(core * half, 128), half)
    other_at = pl.ds(pl.multiple_of((1 - core) * half, 128), half)

    def pair_copy(b):
        return remote(pair_send.at[b], pair_recv.at[b], pair_s.at[b], pair_r.at[b], {"tensor": sibling})

    def far_copy(b):
        return remote(far_send.at[b], far_recv.at[core], far_s.at[b], far_r.at[core], {"tensor": b})

    def near_copy():
        return remote(near_send, near_recv, near_s.at[0], near_r.at[0], {"tensor": sibling})

    def low_copy(b):
        return remote(low_send.at[b], low_recv.at[t], low_s.at[b], low_r.at[t], {"tensor": b})

    def times(b, at):
        return jnp.dot(x[b], wd[:, at], preferred_element_type=jnp.float32)

    def compute(b):
        both = jnp.dot(x[b], wd[:, cols:], preferred_element_type=jnp.float32)
        id_col = column(b)
        zero = jnp.zeros((rows, 2 * rank), jnp.float32)
        low = jnp.where(id_col == 2 * a, both[:, : 2 * rank], zero)
        low = jnp.where(id_col == 2 * a + 1, both[:, 2 * rank :], low)
        low_send[b] = low

        @pl.when(b != t)
        def _():
            low_copy(b).start()

        @pl.when(b // 2 != here)
        def _():
            pair_send[b] = times(b, other_at).astype(jnp.bfloat16)
            pair_copy(b).start()
            held[...] = times(b, mine_at)
            pair_copy(b).wait_recv()
            far_send[b] = (held[...] + pair_recv[b].astype(jnp.float32)).astype(jnp.bfloat16)
            far_copy(b).start()

        @pl.when(b == sibling)
        def _():
            @pl.loop(0, 2)
            def _(n):
                at = pl.ds(pl.multiple_of(n * half, 128), half)
                near_send[:, at] = times(b, at).astype(jnp.bfloat16)

            near_copy().start()

        @pl.when(b == t)
        def _():
            @pl.loop(0, 2)
            def _(n):
                at = pl.ds(pl.multiple_of(n * half, 128), half)
                base[:, at] = times(b, at)

    for copy in loads:
        copy.wait()
    compute(a)

    for s in range(1, ZN):
        lo, hi = a - s, a + s
        for i in range(CHUNKS):
            @pl.when(lo >= 0)
            def _():
                to_right(tok_ref, lo, i).wait_recv()

                @pl.when(a < ZN - 1)
                def _():
                    to_right(x.at[lo], lo, i).start()

            @pl.when(hi < ZN)
            def _():
                to_left(tok_ref, hi, i).wait_recv()

                @pl.when(a > 0)
                def _():
                    to_left(x.at[hi], hi, i).start()

        if s == 2:
            y_in = ball.at[pl.ds(0, ZN - 1), pl.ds(pl.multiple_of((2 * t + 1 - g) * part, part), part), :]
            remote(y_in, y_in, plane_s.at[0], plane_r.at[0], {"groups": 1 - g}).wait_recv()
            x_copy(t).start()

        @pl.loop(0, 2)
        def _(way):
            b = a - s + 2 * s * way

            @pl.when((b >= 0) & (b < ZN))
            def _():
                remote(ids.at[b], ids.at[b], ids_s.at[1], ids_r.at[b], {"adapter": zdev[1]}).wait_recv()
                compute(b)

        if s == 1:
            for d in range(1, ZN):
                bq_copy(d).wait_recv()
                bv_copy(d).wait_recv()
            y_copy().start()
        if s == 3:
            x_copy(xpeer).wait_recv()
            core_copy(0, t).start()
            core_copy(1, xpeer).start()

    total = low_send[t]
    for d in range(1, ZN):
        remote(low_send.at[0], low_recv.at[tdev[d]], low_s.at[0], low_r.at[tdev[d]], {"tensor": tdev[d]}).wait_recv()
        total = total + low_recv[tdev[d]]
    low_z[0] = (total * adapter_scale).astype(jnp.bfloat16)

    def lz_copy(d):
        return remote(low_z.at[0], low_z.at[d], lz_s.at[d], lz_r.at[d], {"adapter": zdev[d]})

    for d in range(1, ZN):
        lz_copy(d).start()
    for copy in owns:
        copy.wait()
    core_copy(0, sibling).wait_recv()
    core_copy(1, lax.rem(sibling + 2, ZN)).wait_recv()
    id_col = column(t)
    low = low_z[0].astype(jnp.float32)
    for d in range(1, ZN):
        lz_copy(d).wait_recv()
        low = low + low_z[d].astype(jnp.float32)
    wide = jnp.concatenate([low[:, :rank], low[:, :rank]], axis=1)
    wide_v = jnp.concatenate([low[:, rank:], low[:, rank:]], axis=1)
    second = lax.broadcasted_iota(jnp.int32, (rows, 2 * rank), 1) // rank
    lq, lv = [], []
    for slot in range(ZN):
        owner = zdev[(ZN - 1 - slot) % ZN]
        hit = id_col == 2 * owner + second
        lq.append(jnp.where(hit, wide, 0.0).astype(jnp.bfloat16))
        lv.append(jnp.where(hit, wide_v, 0.0).astype(jnp.bfloat16))
    lq = jnp.concatenate(lq, axis=1)
    lv = jnp.concatenate(lv, axis=1)
    near_copy().wait_recv()
    for h in range(2):
        remote(far_recv.at[h], far_recv.at[h], far_s.at[0], far_r.at[h], {"tensor": xpeer}).wait_recv()

    def finish(at, low_rows, b_at, width):
        factors = ball[:, :, b_at : b_at + width].reshape(ZN * 2 * rank, width)
        delta = jnp.dot(low_rows, factors, preferred_element_type=jnp.float32)
        val = base[:, at : at + width] + near_recv[:, at : at + width].astype(jnp.float32)
        far = far_recv[at // half, :, at % half : at % half + width]
        val = val + far.astype(jnp.float32)
        delta = delta.astype(jnp.bfloat16).astype(jnp.float32)
        out_ref[:, at : at + width] = (val + delta).astype(jnp.bfloat16)

    for grp in range(groups_here):
        for c in range(qg // 256):
            finish(grp * (qg + vg) + c * 256, lq, grp * qg + c * 256, 256)
        finish(grp * (qg + vg) + qg, lv, qcols + grp * vg, vg)

    @pl.loop(0, ZN)
    def _(b):
        @pl.when((b <= a) & (a < ZN - 1))
        def _():
            for i in range(CHUNKS):
                to_right(tok_ref, b, i).wait_send()

        @pl.when((b >= a) & (a > 0))
        def _():
            for i in range(CHUNKS):
                to_left(tok_ref, b, i).wait_send()

        @pl.when(b != t)
        def _():
            low_copy(b).wait_send()

        @pl.when(b // 2 != here)
        def _():
            pair_copy(b).wait_send()
            far_copy(b).wait_send()

    for d in range(1, ZN):
        ids_copy(d).wait_send()
        bq_copy(d).wait_send()
        bv_copy(d).wait_send()
        lz_copy(d).wait_send()
    near_copy().wait_send()
    y_copy().wait_send()
    x_copy(t).wait_send()
    core_copy(0, t).wait_send()
    core_copy(1, xpeer).wait_send()


def fused_on_device(tokens, weight, down, bq, bv, index_rows):
    rows, feats = tokens.shape
    cols = weight.shape[1]
    rank2 = down.shape[2]
    ids = index_rows[None, :]
    dma = pltpu.SemaphoreType.DMA
    vmem = pltpu.VMEM
    any_spec = pl.BlockSpec(memory_space=pltpu.HBM)
    return pl.pallas_call(
        fused_kernel,
        out_shape=jax.ShapeDtypeStruct((rows, cols), jnp.bfloat16),
        in_specs=[any_spec] * 5 + [pl.BlockSpec(memory_space=pltpu.VMEM)],
        out_specs=pl.BlockSpec(memory_space=pltpu.VMEM),
        scratch_shapes=[
            vmem((ZN, rows, feats), jnp.bfloat16),
            vmem((feats, cols + 2 * rank2), jnp.bfloat16),
            vmem((ZN, rows, cols // 2), jnp.bfloat16),
            vmem((ZN, rows, cols // 2), jnp.bfloat16),
            vmem((ZN, rows, cols // 2), jnp.bfloat16),
            vmem((2, rows, cols // 2), jnp.bfloat16),
            vmem((rows, cols), jnp.bfloat16),
            vmem((rows, cols), jnp.bfloat16),
            vmem((rows, cols // 2), jnp.float32),
            vmem((rows, cols), jnp.float32),
            vmem((ZN, rows, rank2), jnp.float32),
            vmem((ZN, rows, rank2), jnp.float32),
            vmem((ZN, rows, rank2), jnp.bfloat16),
            vmem((ZN, rank2, cols), jnp.bfloat16),
            vmem((ZN, 8, 128), jnp.int32),
        ] + [dma((ZN,))] * 20 + [dma((ZN, CHUNKS))] * 3,
        compiler_params=pltpu.CompilerParams(
            collective_id=0, has_side_effects=True, vmem_limit_bytes=62 * 1024 * 1024
        ),
    )(tokens, weight, down, bq, bv, ids)


def solution(mesh):
    fused = (mesh.shape["groups"], mesh.shape["adapter"], mesh.shape["tensor"]) == (2, ZN, ZN)
    in_specs = (
        P(("groups", "adapter"), "tensor"),
        P("tensor", "adapter"),
        P("adapter", "tensor", None),
        P("adapter", None, None),
        P("adapter", None, None),
        P(("groups", "adapter")),
    )
    out_specs = P(("groups", "tensor"), "adapter")
    return jax.shard_map(
        fused_on_device if fused else on_device,
        mesh=mesh, in_specs=in_specs, out_specs=out_specs, check_vma=False,
    )
```

```python
import jax
import jax.numpy as jnp
from jax import lax
from jax.experimental import pallas as pl
from jax.experimental.pallas import tpu as pltpu
from jax.sharding import PartitionSpec as P

KVHEADS = 8


adapter_scale = 0.5


def slot_table(hit, capacity):
    counts = jnp.cumsum(hit.astype(jnp.int32), axis=-1) - 1
    places = jnp.arange(capacity, dtype=jnp.int32)
    match = hit[..., None, :] & (counts[..., None, :] == places[:, None])
    column = jnp.arange(hit.shape[-1], dtype=jnp.int32)
    row_of = jnp.sum(jnp.where(match, column, 0), axis=-1)
    filled = jnp.any(match, axis=-1)
    return (row_of, filled)


def on_device(
    tokens,
    query_value_weight,
    adapter_down_factors,
    adapter_query_factors,
    adapter_value_factors,
    adapter_index_rows,
):
    owners_n = lax.axis_size("adapter")
    tensor_n = lax.axis_size("tensor")
    owner_self = lax.axis_index("adapter")
    tensor_self = lax.axis_index("tensor")
    row_dev = tokens.shape[0]
    local_row_count = adapter_down_factors.shape[0]
    value_rank_slice = adapter_down_factors.shape[2]
    query_rank_slice = value_rank_slice // 2
    capacity = max(2, min(4 * row_dev // owners_n, row_dev // 2))
    group_src = owners_n // tensor_n
    block_cols = query_value_weight.shape[1]
    all_ids = lax.all_gather(adapter_index_rows, "adapter", axis=0, tiled=True).reshape(
        owners_n, row_dev
    )
    owners_all = all_ids // local_row_count
    gathered = lax.all_gather(tokens, "adapter", axis=0, tiled=True)
    base = lax.psum_scatter(
        jnp.dot(gathered, query_value_weight, preferred_element_type=jnp.float32),
        "tensor",
        scatter_dimension=0,
        tiled=True,
    )
    slot_row, slot_ok = slot_table(owners_all == owner_self, capacity)
    slot_ids = jnp.take_along_axis(all_ids, slot_row, axis=1)
    local_pick = (slot_ids - owner_self * local_row_count)[..., None] == jnp.arange(
        local_row_count, dtype=jnp.int32
    )
    select = (local_pick & slot_ok[..., None]).astype(jnp.float32)
    targets = jnp.arange(owners_n, dtype=jnp.int32)[:, None]
    send_row, send_ok = slot_table(
        (adapter_index_rows // local_row_count)[None, :] == targets, capacity
    )
    outgoing = jnp.where(send_ok[..., None], tokens[send_row], jnp.zeros((), tokens.dtype))
    dense = jnp.einsum(
        "scd,kdq->sckq",
        lax.all_to_all(outgoing, "adapter", split_axis=0, concat_axis=0, tiled=True),
        adapter_down_factors,
        preferred_element_type=jnp.float32,
    )
    partial_low = jnp.sum(dense * select[..., None], axis=2)
    accumulated_sum = lax.psum(partial_low, "tensor")
    accumulated_sum = lax.dynamic_slice_in_dim(
        accumulated_sum, tensor_self * group_src, group_src, 0
    )
    reduced_rows = (accumulated_sum * adapter_scale).astype(jnp.bfloat16)
    mine = lax.dynamic_slice_in_dim(select, tensor_self * group_src, group_src, 0).astype(
        jnp.bfloat16
    )
    slots_n = group_src * capacity
    broadcast_rows = (mine[..., None] * reduced_rows[..., None, :]).reshape(
        slots_n, local_row_count, value_rank_slice
    )
    up_query = jnp.einsum(
        "mwn,wnq->mq",
        broadcast_rows[..., :query_rank_slice],
        adapter_query_factors,
        preferred_element_type=jnp.float32,
    )
    up_value = jnp.einsum(
        "mwn,wnq->mq",
        broadcast_rows[..., query_rank_slice:],
        adapter_value_factors,
        preferred_element_type=jnp.float32,
    )
    delta = jnp.concatenate(
        [
            up_query.astype(jnp.bfloat16).reshape(slots_n, KVHEADS, -1),
            up_value.astype(jnp.bfloat16).reshape(slots_n, KVHEADS, -1),
        ],
        axis=2,
    )
    delta = delta.reshape(slots_n, owners_n, block_cols).transpose(1, 0, 2)
    returned = lax.all_to_all(delta, "adapter", split_axis=0, concat_axis=0, tiled=True).reshape(
        owners_n * slots_n, block_cols
    )
    mine_owner = lax.dynamic_slice_in_dim(owners_all, tensor_self * group_src, group_src, 0)
    owner_hit = mine_owner[:, None, :] == jnp.arange(owners_n, dtype=jnp.int32)[None, :, None]
    running = jnp.cumsum(owner_hit.astype(jnp.int32), axis=-1) - 1
    place = jnp.sum(jnp.where(owner_hit, running, 0), axis=1)
    source_off = jnp.arange(group_src, dtype=jnp.int32)[:, None] * capacity
    lookup = (mine_owner * slots_n + source_off + place).reshape(-1)
    delta_rows = jnp.take(returned, lookup, axis=0)
    return (base + delta_rows.astype(jnp.float32)).astype(jnp.bfloat16)


MESH = pl.DeviceIdType.MESH
CHUNKS = 3
ZN = 4


def remote(src, dst, send_sem, recv_sem, device):
    return pltpu.make_async_remote_copy(
        src_ref=src,
        dst_ref=dst,
        send_sem=send_sem,
        recv_sem=recv_sem,
        device_id=device,
        device_id_type=MESH,
    )


def fused_kernel(
    tok_ref, w_ref, down_ref, bq_ref, bv_ref, ids_ref, out_ref,
    x, wd, pair_send, pair_recv, far_send, far_recv, near_send, near_recv, held, base, low_send, low_recv, low_z, ball, ids,
    load_sem, own_sem, ids_s, ids_r, pair_s, far_s, far_r, near_s, near_r,
    low_s, low_r, lz_s, lz_r, bqz_s, bqz_r, bvz_s, bvz_r, plane_s, plane_r, right_s, left_s, x_r, pair_r,
):
    g = lax.axis_index("groups")
    a = lax.axis_index("adapter")
    t = lax.axis_index("tensor")
    cols = w_ref.shape[1]
    qcols = bq_ref.shape[2] // ZN
    vcols = bv_ref.shape[2] // ZN
    rank = bq_ref.shape[1]
    rows = tok_ref.shape[0]
    groups_here = KVHEADS // ZN
    qg, vg = qcols // groups_here, vcols // groups_here
    zdev = [lax.rem(a + d, ZN) for d in range(ZN)]
    tdev = [lax.rem(t + d, ZN) for d in range(ZN)]
    xpeer = lax.rem(t + 2, ZN)
    core = lax.rem(t, 2)
    sibling = t + 1 - 2 * core

    loads = [
        pltpu.make_async_copy(w_ref, wd.at[:, pl.ds(0, cols)], load_sem.at[0]),
        pltpu.make_async_copy(down_ref.at[0], wd.at[:, pl.ds(cols, 2 * rank)], load_sem.at[1]),
        pltpu.make_async_copy(
            down_ref.at[1], wd.at[:, pl.ds(cols + 2 * rank, 2 * rank)], load_sem.at[2]
        ),
        pltpu.make_async_copy(tok_ref, x.at[a], load_sem.at[3]),
    ]
    for copy in loads:
        copy.start()
    own_q = pl.ds(pl.multiple_of(a * qcols, 128), qcols)
    own_v = pl.ds(pl.multiple_of(a * vcols, 128), vcols)
    owns = []
    for k in range(2):
        at = pl.ds(k * rank, rank)
        owns.append(pltpu.make_async_copy(
            bq_ref.at[k, :, own_q], ball.at[ZN - 1, at, pl.ds(0, qcols)], own_sem.at[2 * k]))
        owns.append(pltpu.make_async_copy(
            bv_ref.at[k, :, own_v], ball.at[ZN - 1, at, pl.ds(qcols, vcols)], own_sem.at[2 * k + 1]))
    for copy in owns:
        copy.start()
    ids[a] = jnp.zeros((8, 128), jnp.int32)
    ids[a, 0:1, 0:rows] = ids_ref[...]

    barrier = pltpu.get_barrier_semaphore()
    for d in range(1, ZN):
        pl.semaphore_signal(barrier, inc=1, device_id={"adapter": zdev[d]}, device_id_type=MESH)
        pl.semaphore_signal(barrier, inc=1, device_id={"tensor": tdev[d]}, device_id_type=MESH)
    pl.semaphore_signal(barrier, inc=1, device_id={"groups": 1 - g}, device_id_type=MESH)
    pl.semaphore_wait(barrier, 2 * ZN - 1)

    part = ball.shape[1] // (2 * ZN)
    p = 2 * t + g
    p_rows = pl.ds(pl.multiple_of(p * part, part), part)
    k_src = t // 2
    r_src = pl.ds(pl.multiple_of((2 * core + g) * part, part), part)

    def ids_copy(d):
        return remote(ids.at[a], ids.at[a], ids_s.at[d], ids_r.at[a], {"adapter": zdev[d]})

    def bq_copy(d):
        at = pl.ds(pl.multiple_of(zdev[d] * qcols, 128), qcols)
        return remote(bq_ref.at[k_src, r_src, at], ball.at[d - 1, p_rows, pl.ds(0, qcols)],
                      bqz_s.at[d], bqz_r.at[d], {"adapter": zdev[d]})

    def bv_copy(d):
        at = pl.ds(pl.multiple_of(zdev[d] * vcols, 128), vcols)
        return remote(bv_ref.at[k_src, r_src, at], ball.at[d - 1, p_rows, pl.ds(qcols, vcols)],
                      bvz_s.at[d], bvz_r.at[d], {"adapter": zdev[d]})

    for d in range(1, ZN):
        ids_copy(d).start()
    for d in range(1, ZN):
        bq_copy(d).start()
        bv_copy(d).start()

    step = rows // CHUNKS

    def to_right(src, b, i):
        at = pl.ds(i * step, step)
        return remote(src.at[at], x.at[b, at], right_s.at[b, i], x_r.at[b, i],
                      {"adapter": lax.rem(a + 1, ZN)})

    def to_left(src, b, i):
        at = pl.ds(i * step, step)
        return remote(src.at[at], x.at[b, at], left_s.at[b, i], x_r.at[b, i],
                      {"adapter": lax.rem(a + ZN - 1, ZN)})

    for i in range(CHUNKS):
        @pl.when(a < ZN - 1)
        def _():
            to_right(tok_ref, a, i).start()

        @pl.when(a > 0)
        def _():
            to_left(tok_ref, a, i).start()

    def y_copy():
        ref = ball.at[pl.ds(0, ZN - 1), p_rows, :]
        return remote(ref, ref, plane_s.at[0], plane_r.at[0], {"groups": 1 - g})

    def t_rows(owner_t):
        return ball.at[pl.ds(0, ZN - 1), pl.ds(pl.multiple_of(owner_t * 2 * part, 2 * part), 2 * part), :]

    def x_copy(owner_t):
        ref = t_rows(owner_t)
        return remote(ref, ref, plane_s.at[1], plane_r.at[1], {"tensor": xpeer})

    def core_copy(i, owner_t):
        ref = t_rows(owner_t)
        return remote(ref, ref, plane_s.at[2 + i], plane_r.at[2 + i], {"tensor": sibling})

    def column(b):
        lane = lax.broadcasted_iota(jnp.int32, (rows, 128), 1)
        row = lax.broadcasted_iota(jnp.int32, (rows, 128), 0)
        ids_b = jnp.broadcast_to(ids[b][0:1, :], (rows, 128))
        return jnp.sum(jnp.where(lane == row, ids_b, 0), axis=1, keepdims=True)

    half = cols // 2
    here = t // 2
    mine_at = pl.ds(pl.multiple_of(core * half, 128), half)
    other_at = pl.ds(pl.multiple_of((1 - core) * half, 128), half)

    def pair_copy(b, at, piece):
        return remote(pair_send.at[b, at], pair_recv.at[b, at], pair_s.at[b], pair_r.at[b, piece],
                      {"tensor": sibling})

    def far_copy(b, at):
        return remote(far_send.at[b, at], far_recv.at[core, at], far_s.at[b], far_r.at[core],
                      {"tensor": b})

    def near_copy():
        return remote(near_send, near_recv, near_s.at[0], near_r.at[0], {"tensor": sibling})

    def low_copy(b):
        return remote(low_send.at[b], low_recv.at[t], low_s.at[b], low_r.at[t], {"tensor": b})

    whole = pl.ds(0, rows)

    def compute(b, r0, n, piece):
        at_rows = pl.ds(r0, n)
        last = r0 + n == rows

        def times(at):
            return jnp.dot(x[b, at_rows], wd[:, at], preferred_element_type=jnp.float32)

        both = times(pl.ds(cols, 4 * rank))
        id_col = column(b)[r0 : r0 + n]
        zero = jnp.zeros((n, 2 * rank), jnp.float32)
        low = jnp.where(id_col == 2 * a, both[:, : 2 * rank], zero)
        low = jnp.where(id_col == 2 * a + 1, both[:, 2 * rank :], low)
        low_send[b, at_rows] = low

        if last:
            @pl.when(b != t)
            def _():
                low_copy(b).start()

        @pl.when(b // 2 != here)
        def _():
            pair_send[b, at_rows] = times(other_at).astype(jnp.bfloat16)
            pair_copy(b, at_rows, piece).start()
            held[at_rows] = times(mine_at)
            pair_copy(b, at_rows, piece).wait_recv()
            far_send[b, at_rows] = (
                held[at_rows] + pair_recv[b, at_rows].astype(jnp.float32)
            ).astype(jnp.bfloat16)
            far_copy(b, at_rows).start()

        @pl.when(b == sibling)
        def _():
            @pl.loop(0, 2)
            def _(m):
                at = pl.ds(pl.multiple_of(m * half, 128), half)
                near_send[at_rows, at] = times(at).astype(jnp.bfloat16)

            if last:
                near_copy().start()

        @pl.when(b == t)
        def _():
            @pl.loop(0, 2)
            def _(m):
                at = pl.ds(pl.multiple_of(m * half, 128), half)
                base[at_rows, at] = times(at)

    for copy in loads:
        copy.wait()
    compute(a, 0, rows, 0)

    for d in range(1, ZN):
        bq_copy(d).wait_recv()
        bv_copy(d).wait_recv()
    y_copy().start()

    for s in range(1, ZN - 1):
        lo, hi = a - s, a + s
        for i in range(CHUNKS):
            @pl.when(lo >= 0)
            def _():
                to_right(tok_ref, lo, i).wait_recv()

                @pl.when(a < ZN - 1)
                def _():
                    to_right(x.at[lo], lo, i).start()

            @pl.when(hi < ZN)
            def _():
                to_left(tok_ref, hi, i).wait_recv()

                @pl.when(a > 0)
                def _():
                    to_left(x.at[hi], hi, i).start()

        if s == 1:
            y_in = ball.at[pl.ds(0, ZN - 1), pl.ds(pl.multiple_of((2 * t + 1 - g) * part, part), part), :]
            remote(y_in, y_in, plane_s.at[0], plane_r.at[0], {"groups": 1 - g}).wait_recv()
            x_copy(t).start()
            core_copy(0, t).start()

        @pl.loop(0, 2)
        def _(way):
            b = a - s + 2 * s * way

            @pl.when((b >= 0) & (b < ZN))
            def _():
                remote(ids.at[b], ids.at[b], ids_s.at[1], ids_r.at[b], {"adapter": zdev[1]}).wait_recv()
                compute(b, 0, rows, 0)


    x_copy(xpeer).wait_recv()
    core_copy(1, xpeer).start()

    far_end = ZN - 1 - a

    @pl.when((a == 0) | (a == ZN - 1))
    def _():
        remote(ids.at[far_end], ids.at[far_end], ids_s.at[1], ids_r.at[far_end],
               {"adapter": zdev[1]}).wait_recv()
        for i in range(CHUNKS):
            to_left(tok_ref, far_end, i).wait_recv()
        compute(far_end, 0, rows, 0)

    total = low_send[t]
    for d in range(1, ZN):
        remote(low_send.at[0], low_recv.at[tdev[d]], low_s.at[0], low_r.at[tdev[d]], {"tensor": tdev[d]}).wait_recv()
        total = total + low_recv[tdev[d]]
    low_z[0] = (total * adapter_scale).astype(jnp.bfloat16)

    def lz_copy(d):
        return remote(low_z.at[0], low_z.at[d], lz_s.at[d], lz_r.at[d], {"adapter": zdev[d]})

    for d in range(1, ZN):
        lz_copy(d).start()
    for copy in owns:
        copy.wait()
    core_copy(0, sibling).wait_recv()
    core_copy(1, lax.rem(sibling + 2, ZN)).wait_recv()
    id_col = column(t)
    low = low_z[0].astype(jnp.float32)
    for d in range(1, ZN):
        lz_copy(d).wait_recv()
        low = low + low_z[d].astype(jnp.float32)
    wide = jnp.concatenate([low[:, :rank], low[:, :rank]], axis=1)
    wide_v = jnp.concatenate([low[:, rank:], low[:, rank:]], axis=1)
    second = lax.broadcasted_iota(jnp.int32, (rows, 2 * rank), 1) // rank
    lq, lv = [], []
    for slot in range(ZN):
        owner = zdev[(ZN - 1 - slot) % ZN]
        hit = id_col == 2 * owner + second
        lq.append(jnp.where(hit, wide, 0.0).astype(jnp.bfloat16))
        lv.append(jnp.where(hit, wide_v, 0.0).astype(jnp.bfloat16))
    lq = jnp.concatenate(lq, axis=1)
    lv = jnp.concatenate(lv, axis=1)
    near_copy().wait_recv()

    def add_delta(at, low_rows, b_at, width):
        factors = ball[:, :, b_at : b_at + width].reshape(ZN * 2 * rank, width)
        delta = jnp.dot(low_rows, factors, preferred_element_type=jnp.float32)
        delta = delta.astype(jnp.bfloat16).astype(jnp.float32)
        near = near_recv[:, at : at + width].astype(jnp.float32)
        base[:, at : at + width] = base[:, at : at + width] + near + delta

    for grp in range(groups_here):
        for c in range(qg // 256):
            add_delta(grp * (qg + vg) + c * 256, lq, grp * qg + c * 256, 256)
        add_delta(grp * (qg + vg) + qg, lv, qcols + grp * vg, vg)

    for h in range(2):
        remote(far_recv.at[h], far_recv.at[h], far_s.at[0], far_r.at[h], {"tensor": xpeer}).wait_recv()
        at = pl.ds(h * half, half)
        out_ref[:, at] = (base[:, at] + far_recv[h].astype(jnp.float32)).astype(jnp.bfloat16)

    @pl.loop(0, ZN)
    def _(b):
        @pl.when((b <= a) & (a < ZN - 1))
        def _():
            for i in range(CHUNKS):
                to_right(tok_ref, b, i).wait_send()

        @pl.when((b >= a) & (a > 0))
        def _():
            for i in range(CHUNKS):
                to_left(tok_ref, b, i).wait_send()

        @pl.when(b != t)
        def _():
            low_copy(b).wait_send()

        @pl.when(b // 2 != here)
        def _():
            pair_copy(b, whole, 0).wait_send()
            far_copy(b, whole).wait_send()

    for d in range(1, ZN):
        ids_copy(d).wait_send()
        bq_copy(d).wait_send()
        bv_copy(d).wait_send()
        lz_copy(d).wait_send()
    near_copy().wait_send()
    y_copy().wait_send()
    x_copy(t).wait_send()
    core_copy(0, t).wait_send()
    core_copy(1, xpeer).wait_send()


def fused_on_device(tokens, weight, down, bq, bv, index_rows):
    rows, feats = tokens.shape
    cols = weight.shape[1]
    rank2 = down.shape[2]
    ids = index_rows[None, :]
    dma = pltpu.SemaphoreType.DMA
    vmem = pltpu.VMEM
    any_spec = pl.BlockSpec(memory_space=pltpu.HBM)
    return pl.pallas_call(
        fused_kernel,
        out_shape=jax.ShapeDtypeStruct((rows, cols), jnp.bfloat16),
        in_specs=[any_spec] * 5 + [pl.BlockSpec(memory_space=pltpu.VMEM)],
        out_specs=pl.BlockSpec(memory_space=pltpu.VMEM),
        scratch_shapes=[
            vmem((ZN, rows, feats), jnp.bfloat16),
            vmem((feats, cols + 2 * rank2), jnp.bfloat16),
            vmem((ZN, rows, cols // 2), jnp.bfloat16),
            vmem((ZN, rows, cols // 2), jnp.bfloat16),
            vmem((ZN, rows, cols // 2), jnp.bfloat16),
            vmem((2, rows, cols // 2), jnp.bfloat16),
            vmem((rows, cols), jnp.bfloat16),
            vmem((rows, cols), jnp.bfloat16),
            vmem((rows, cols // 2), jnp.float32),
            vmem((rows, cols), jnp.float32),
            vmem((ZN, rows, rank2), jnp.float32),
            vmem((ZN, rows, rank2), jnp.float32),
            vmem((ZN, rows, rank2), jnp.bfloat16),
            vmem((ZN, rank2, cols), jnp.bfloat16),
            vmem((ZN, 8, 128), jnp.int32),
        ] + [dma((ZN,))] * 19 + [dma((ZN, CHUNKS))] * 4,
        compiler_params=pltpu.CompilerParams(
            collective_id=0, has_side_effects=True, vmem_limit_bytes=62 * 1024 * 1024
        ),
    )(tokens, weight, down, bq, bv, ids)


def solution(mesh):
    fused = (mesh.shape["groups"], mesh.shape["adapter"], mesh.shape["tensor"]) == (2, ZN, ZN)
    in_specs = (
        P(("groups", "adapter"), "tensor"),
        P("tensor", "adapter"),
        P("adapter", "tensor", None),
        P("adapter", None, None),
        P("adapter", None, None),
        P(("groups", "adapter")),
    )
    out_specs = P(("groups", "tensor"), "adapter")
    return jax.shard_map(
        fused_on_device if fused else on_device,
        mesh=mesh, in_specs=in_specs, out_specs=out_specs, check_vma=False,
    )
```
